32 devices in a mesh: dp: 8 (over z, y), row: 2 (over x), col: 2 (over core).
Axes of the slice: x: 2, y: 2, z: 4, core: 2. Of those that a mesh axis runs over, the one named last changes fastest.
Arguments:
- inputs: bfloat16 [48, 512, 960], P('dp', 'col', 'row'), may hold values from -6 to 6
- segments: int32 [48, 512], P('dp'), may hold values from 0 to 2, as said below
- positions: int32 [48, 512], P('dp'), may hold values from 0 to 511, as said below
- gain_first: float32 [960], P('row'), may hold values from 0.5 to 1.5
- query_weight: bfloat16 [960, 960], P(('row', 'col')), may hold values from -0.1875 to 0.1875
- key_weight: bfloat16 [960, 320], P(('row', 'col')), may hold values from -0.1875 to 0.1875
- value_weight: bfloat16 [960, 320], P(('row', 'col')), may hold values from -0.1875 to 0.1875
- output_weight: bfloat16 [960, 960], P(('row', 'col')), may hold values from -0.5 to 0.5
- gain_second: float32 [960], P('row'), may hold values from 0.5 to 1.5
- gate_weight: bfloat16 [960, 2560], P('row', 'col'), may hold values from -0.1875 to 0.1875
- up_weight: bfloat16 [960, 2560], P('row', 'col'), may hold values from -0.1875 to 0.1875
- down_weight: bfloat16 [2560, 960], P('col', 'row'), may hold values from -0.25 to 0.25
- cotangent: bfloat16 [48, 512, 960], P('dp', 'col', 'row'), may hold values from -6 to 6
Outputs:
- layer_out: bfloat16 [48, 512, 960], P('dp', 'col', 'row')
- input_grad: float32 [48, 512, 960], P('dp', 'col', 'row')
- gain_first_grad: float32 [960], P('row')
- query_grad: float32 [960, 960], P(('row', 'col'))
- key_grad: float32 [960, 320], P(('row', 'col'))
- value_grad: float32 [960, 320], P(('row', 'col'))
- output_grad: float32 [960, 960], P(('row', 'col'))
- gain_second_grad: float32 [960], P('row')
- gate_grad: float32 [960, 2560], P('row', 'col')
- up_grad: float32 [960, 2560], P('row', 'col')
- down_grad: float32 [2560, 960], P('col', 'row')
The draws below stay inside these ranges and needn't reach their ends.
Inputs may be any that keep to these rules, and one draw needn't show every extreme that they name: `segments`: within a sequence the segment numbers start at 0 and never fall; in the 6 sequences of each index of dp one sequence is a single segment and another holds three. `positions`: each token's offset from the first token of its segment in its sequence.
All inputs are finite; a program needn't handle non-finite values.
Results may differ from the reference program's by a relative error of at most 0.02.
Values may be sent and summed in bfloat16 or wider, within the bound.
A program may use at most 192 MiB of HBM per device.

```python
import jax
import jax.numpy as jnp
from jax import lax

D = 960
QH = 15
KH = 5
HD = 64
FF = 2560
L = 512
SEQS = 6
QD = 960
KD = 320
SEQUENCES = 48
N_DP = 8


def document_cuts(key):
    first_key, second_key, pick_key, shift_key = jax.random.split(key, 4)
    first_cut = jax.random.randint(first_key, (SEQUENCES,), 1, L)
    second_cut = first_cut + jax.random.randint(second_key, (SEQUENCES,), 2 * L // 5, 4 * L)
    chosen = jax.random.randint(pick_key, (SEQUENCES // SEQS,), 0, SEQS)
    seq_index = jnp.arange(SEQUENCES, dtype=jnp.int32)
    group_pick = jnp.repeat(chosen, SEQS)
    local_slot = seq_index % SEQS
    whole_seq = local_slot == group_pick
    split_seq = local_slot == (group_pick + 1) % SEQS
    forced = jax.random.randint(shift_key, (SEQUENCES,), 1, L - 2 * L // 5)
    first_cut = jnp.where(whole_seq, L, jnp.where(split_seq, forced, first_cut))
    second_cut = jnp.where(whole_seq, 2 * L, jnp.where(split_seq, forced + 2 * L // 5, second_cut))
    return (first_cut, second_cut)


def draw_segments(key, part):
    first_cut, second_cut = document_cuts(key)
    token_index = jnp.arange(L, dtype=jnp.int32)[None, :]
    return (token_index >= first_cut[:, None]).astype(jnp.int32) + (token_index >= second_cut[:, None]).astype(jnp.int32)


def draw_positions(key, part):
    first_cut, second_cut = document_cuts(key)
    token_index = jnp.arange(L, dtype=jnp.int32)[None, :]
    seg_start = jnp.where(token_index >= second_cut[:, None], second_cut[:, None], jnp.where(token_index >= first_cut[:, None], first_cut[:, None], 0))
    return (token_index - seg_start).astype(jnp.int32)


def steps_of(key, extent, pieces, low, top_value):
    def one(position, blocks):
        steps = jax.random.uniform(jax.random.fold_in(jax.random.fold_in(key, 6), position), (blocks,), jnp.float32, low / len(pieces), top_value / len(pieces))
        return jnp.repeat(jnp.exp(steps), extent[position] // blocks).reshape((-1,) + (1,) * (len(extent) - position - 1))

    loudness = one(*pieces[0])
    for cut in pieces[1:]:
        loudness = loudness * one(*cut)
    return loudness


def bell_draw(rng, extent, width, bound, cuts=(), kind=jnp.bfloat16):
    result = jax.random.normal(rng, extent, jnp.float32) * width
    if len(cuts) > 0:
        result = steps_of(rng, extent, cuts, -0.22, 0.18) * result
    return jnp.clip(result, min=-bound, max=bound).astype(kind)


def setup_inputs(seed: int = 0) -> dict:
    arg_keys = jax.random.split(jax.random.key(seed), 14)
    return {
        "inputs": bell_draw(arg_keys[0], (SEQUENCES, L, D), 1.0, 6.0, ((0, 8), (1, 2), (2, 2))),
        "segments": draw_segments(jax.random.fold_in(arg_keys[13], 71), 0),
        "positions": draw_positions(jax.random.fold_in(arg_keys[13], 71), 0),
        "gain_first": jnp.clip(1.0 + 0.1 * jax.random.normal(arg_keys[3], (D,), jnp.float32), 0.5, 1.5),
        "query_weight": bell_draw(arg_keys[4], (D, QD), D ** -0.5, 0.1875, ((0, 4),)),
        "key_weight": bell_draw(arg_keys[5], (D, KD), D ** -0.5, 0.1875, ((0, 4),)),
        "value_weight": bell_draw(arg_keys[6], (D, KD), D ** -0.5, 0.1875, ((0, 4),)),
        "output_weight": bell_draw(arg_keys[7], (QD, D), (QD // 8) ** -0.5, 0.5, ((0, 4),)),
        "gain_second": jnp.clip(1.0 + 0.1 * jax.random.normal(arg_keys[8], (D,), jnp.float32), 0.5, 1.5),
        "gate_weight": bell_draw(arg_keys[9], (D, FF), D ** -0.5, 0.1875, ((0, 2), (1, 2))),
        "up_weight": bell_draw(arg_keys[10], (D, FF), D ** -0.5, 0.1875, ((0, 2), (1, 2))),
        "down_weight": bell_draw(arg_keys[11], (FF, D), (FF // 4) ** -0.5, 0.25, ((0, 2), (1, 2))),
        "cotangent": bell_draw(arg_keys[12], (SEQUENCES, L, D), 1.0, 6.0, ((0, 8), (1, 2), (2, 2))),
    }


@jax.custom_vjp
def low(v):
    return lax.optimization_barrier(v.astype(jnp.bfloat16)).astype(jnp.float32)

@jax.custom_vjp
def low_back(v):
    return v

def low_keep(v):
    return (low(v), None)

def low_pass(kept, grad):
    return (grad,)

def back_keep(v):
    return (v, None)

def back_low(kept, grad):
    return (low(grad),)
low.defvjp(low_keep, low_pass)
low_back.defvjp(back_keep, back_low)
eps_norm = 1e-05
rope_base = 10000.0
precise = lax.Precision.HIGHEST

def matmul(left, right):
    return jnp.matmul(left, right, precision=precise)

def rms_norm(values, gain):
    mean_sq = lax.optimization_barrier(jnp.mean(values * values, axis=-1, keepdims=True))
    return values * lax.rsqrt(mean_sq + eps_norm) * gain

def rotary(pos_block):
    frequency = rope_base ** (-(jnp.arange(HD // 2, dtype=jnp.float32) * 2.0 / HD))
    angle_grid = pos_block.astype(jnp.float32)[..., None] * frequency
    return (jnp.cos(angle_grid)[:, :, None, :], jnp.sin(angle_grid)[:, :, None, :])

def rotate(values, cosine, sine_term):
    half_dim = values.shape[-1] // 2
    lead_half = values[..., :half_dim]
    tail_half = values[..., half_dim:]
    return jnp.concatenate([lead_half * cosine - tail_half * sine_term, tail_half * cosine + lead_half * sine_term], axis=-1)

def block_forward(block_rows, seg_block, pos_block, params):
    gain_first, query_weight, key_weight, value_weight, output_weight, gain_second, gate_weight, up_weight, down_weight = params
    seq_count = block_rows.shape[0]
    normed_first = low_back(low(rms_norm(block_rows, gain_first)))
    query_lin = low_back(matmul(normed_first, query_weight))
    key_lin = low_back(matmul(normed_first, key_weight))
    value_rows = low_back(low(matmul(normed_first, value_weight)))
    cosine, sine_term = rotary(pos_block)
    query_rot = low(rotate(query_lin.reshape(seq_count, L, QH, HD), cosine, sine_term))
    key_rot = low(rotate(key_lin.reshape(seq_count, L, KH, HD), cosine, sine_term))
    query_grp = query_rot.reshape(seq_count, L, KH, QH // KH, HD)
    value_grp = value_rows.reshape(seq_count, L, KH, HD)
    scores = jnp.einsum('sqhgd,skhd->shgqk', query_grp, key_rot, precision=precise) * HD ** (-0.5)
    scores = low_back(scores)
    token_index = jnp.arange(L, dtype=jnp.int32)
    allowed = (seg_block[:, :, None] == seg_block[:, None, :]) & (token_index[None, :, None] >= token_index[None, None, :])
    scores = jnp.where(allowed[:, None, None], scores, -1e+30)
    attn_probs = low(jax.nn.softmax(scores, axis=-1))
    attended = jnp.einsum('shgqk,skhd->sqhgd', attn_probs, value_grp, precision=precise)
    attended = low_back(low(attended.reshape(seq_count, L, QD)))
    branch = low_back(low(matmul(attended, output_weight)))
    middle = block_rows + branch
    normed_second = low_back(low(rms_norm(middle, gain_second)))
    gate_lin = low_back(matmul(normed_second, gate_weight))
    up_lin = low_back(matmul(normed_second, up_weight))
    hidden = low(jax.nn.silu(gate_lin) * up_lin)
    ffn_out = low_back(low(matmul(hidden, down_weight)))
    return middle + ffn_out

def reference(inputs, segments, positions, gain_first, query_weight, key_weight, value_weight, output_weight, gain_second, gate_weight, up_weight, down_weight, cotangent):
    params = tuple((item.astype(jnp.float32) for item in (gain_first, query_weight, key_weight, value_weight, output_weight, gain_second, gate_weight, up_weight, down_weight)))
    stream = inputs.astype(jnp.float32).reshape(N_DP, SEQS, L, D)
    seg_blocks = segments.reshape(N_DP, SEQS, L)
    pos_blocks = positions.reshape(N_DP, SEQS, L)

    def layer_forward(stream_rows, layer_params):
        block_step = jax.checkpoint(lambda block_items: block_forward(block_items[0], block_items[1], block_items[2], layer_params))
        return lax.map(block_step, (stream_rows, seg_blocks, pos_blocks))
    layer_out, pullback = jax.vjp(layer_forward, stream, params)
    input_grad, param_grads = pullback(cotangent.astype(jnp.float32).reshape(stream.shape))
    full_shape = (SEQUENCES, L, D)
    return (layer_out.reshape(full_shape).astype(jnp.bfloat16), input_grad.reshape(full_shape), param_grads[0], param_grads[1], param_grads[2], param_grads[3], param_grads[4], param_grads[5], param_grads[6], param_grads[7], param_grads[8])
```

```python
import jax
import jax.numpy as jnp
from jax import lax
from jax.sharding import PartitionSpec as P

D = 960
QH = 15
KH = 5
HD = 64
QD = 960
KD = 320


eps_norm = 1e-05
rope_base = 10000.0
masked_value = -1e30


def swap(values, axis_name):
    size = lax.axis_size(axis_name)
    return lax.ppermute(values, axis_name, [(i, size - 1 - i) for i in range(size)])


def ordered(own, other, index, axis):
    return jnp.where(
        index == 0,
        jnp.concatenate([own, other], axis=axis),
        jnp.concatenate([other, own], axis=axis),
    )


def half_of(values, index, axis):
    size = values.shape[axis] // 2
    return lax.dynamic_slice_in_dim(values, index * size, size, axis)


def to_tokens(values, row_index):
    other = swap(half_of(values, 1 - row_index, 1), "row")
    return ordered(half_of(values, row_index, 1), other, row_index, 2)


def to_features(values, row_index):
    other = swap(half_of(values, 1 - row_index, 2), "row")
    return ordered(half_of(values, row_index, 2), other, row_index, 1)


def gather_rows(own, row_index, col_index):
    pair = ordered(own[None], swap(own, "row")[None], row_index, 0)
    full = ordered(pair[:, None], swap(pair, "col")[:, None], col_index, 1)
    return full.reshape(-1, own.shape[1])


def scatter_rows(part, row_index, col_index):
    blocks = part.reshape(2, 2, part.shape[0] // 4, part.shape[1])
    keep = half_of(blocks, col_index, 1)[:, 0]
    away = half_of(blocks, 1 - col_index, 1)[:, 0]
    pair = keep + swap(away.astype(jnp.bfloat16), "col").astype(jnp.float32)
    own = half_of(pair, row_index, 0)[0]
    send = half_of(pair, 1 - row_index, 0)[0]
    return own + swap(send.astype(jnp.bfloat16), "row").astype(jnp.float32)


def dp_total(values, dim):
    part = lax.psum_scatter(
        values.astype(jnp.bfloat16), "dp", scatter_dimension=dim, tiled=True
    )
    return lax.all_gather(part, "dp", axis=dim, tiled=True)


def norm_apply(values, gain):
    inv_root = lax.rsqrt(jnp.mean(values * values, axis=-1, keepdims=True) + eps_norm)
    return ((values * inv_root * gain).astype(jnp.bfloat16), inv_root)


def norm_back(values, inv_root, gain, grad_normed):
    weighted = grad_normed * gain
    cross = jnp.sum(weighted * values, axis=-1, keepdims=True)
    grad_values = inv_root * weighted - values * inv_root**3 * cross / D
    gain_part = jnp.sum(grad_normed * values * inv_root, axis=(0, 1))
    return (grad_values, gain_part)


def dot(spec, left, right):
    return jnp.einsum(spec, left, right, preferred_element_type=jnp.float32)


def rotary(pos_rows):
    frequency = rope_base ** (-(jnp.arange(HD // 2, dtype=jnp.float32) * 2.0 / HD))
    angle_grid = pos_rows.astype(jnp.float32)[..., None] * frequency
    return (jnp.cos(angle_grid)[:, :, None, :], jnp.sin(angle_grid)[:, :, None, :])


def rotate(values, cosine, sine_term):
    half_dim = values.shape[-1] // 2
    lead_half = values[..., :half_dim]
    tail_half = values[..., half_dim:]
    return jnp.concatenate(
        [lead_half * cosine - tail_half * sine_term, tail_half * cosine + lead_half * sine_term],
        axis=-1,
    )


def unrotate(grads, cosine, sine_term):
    half_dim = grads.shape[-1] // 2
    lead_half = grads[..., :half_dim]
    tail_half = grads[..., half_dim:]
    return jnp.concatenate(
        [lead_half * cosine + tail_half * sine_term, tail_half * cosine - lead_half * sine_term],
        axis=-1,
    )


def masked_scores(query_grp, key_rows, allowed):
    scores = jnp.einsum(
        "sqhgd,skhd->shgqk", query_grp, key_rows, preferred_element_type=jnp.float32
    ) * HD ** (-0.5)
    return jnp.where(allowed[:, None, None], scores, masked_value)


def split_kv(kv_rows, seq_count, length):
    key_rows = kv_rows[..., :KD].reshape(seq_count, length, KH, HD)
    value_rows = kv_rows[..., KD:].reshape(seq_count, length, KH, HD)
    return (key_rows, value_rows)


def local(
    inputs,
    segments,
    positions,
    gain_first,
    query_weight,
    key_weight,
    value_weight,
    output_weight,
    gain_second,
    gate_weight,
    up_weight,
    down_weight,
    cotangent,
):
    seq_count, half_len, half_width = inputs.shape
    length = segments.shape[1]
    quarter = length // 4
    own_rows = seq_count * quarter
    dp_size = lax.axis_size("dp")
    dp_index = lax.axis_index("dp")
    row_index = lax.axis_index("row")
    col_index = lax.axis_index("col")
    bf16 = jnp.bfloat16

    x_tok = to_tokens(inputs, row_index).astype(jnp.float32)
    qkv_full = gather_rows(
        jnp.concatenate([query_weight, key_weight, value_weight], axis=1), row_index, col_index
    )

    own_ffn = jnp.stack([gate_weight.T, up_weight.T, down_weight])
    units = own_ffn.shape[1]
    piece = units // dp_size
    ffn_slice = jnp.stack(
        [
            lax.dynamic_slice_in_dim(gate_weight, dp_index * piece, piece, 1).T,
            lax.dynamic_slice_in_dim(up_weight, dp_index * piece, piece, 1).T,
            lax.dynamic_slice_in_dim(down_weight, dp_index * piece, piece, 0),
        ]
    )
    other_ffn = lax.all_gather(swap(ffn_slice, "row"), "dp", axis=1, tiled=True)
    ffn_full = ordered(own_ffn, other_ffn, row_index, 2)
    gate_full, up_full, down_full = ffn_full[0], ffn_full[1], ffn_full[2]
    output_full = gather_rows(output_weight, row_index, col_index)
    gain_own = jnp.stack([gain_first, gain_second])
    gain_full = ordered(gain_own, swap(gain_own, "row"), row_index, 1)
    dy_own = to_tokens(cotangent, row_index)

    starts = [
        (c * 2 + r) * quarter
        for c, r in (
            (col_index, row_index),
            (col_index, 1 - row_index),
            (1 - col_index, row_index),
            (1 - col_index, 1 - row_index),
        )
    ]
    span = jnp.arange(quarter, dtype=jnp.int32)
    query_pos = lax.dynamic_slice_in_dim(positions, starts[0], quarter, 1)
    query_seg = lax.dynamic_slice_in_dim(segments, starts[0], quarter, 1)
    key_seg = jnp.concatenate(
        [lax.dynamic_slice_in_dim(segments, s, quarter, 1) for s in starts], axis=1
    )
    key_order = jnp.concatenate([s + span for s in starts])
    query_order = starts[0] + span
    allowed = (query_seg[:, :, None] == key_seg[:, None, :]) & (
        key_order[None, None, :] <= query_order[None, :, None]
    )

    first_tok, root_first = norm_apply(x_tok, gain_full[0])
    qkv_lin = dot("sqd,de->sqe", first_tok, qkv_full)
    cosine, sine_term = rotary(query_pos)
    key_rot = rotate(
        qkv_lin[..., QD : QD + KD].reshape(seq_count, quarter, KH, HD), cosine, sine_term
    ).astype(bf16)
    kv_own = jnp.concatenate(
        [key_rot.reshape(seq_count, quarter, KD), qkv_lin[..., QD + KD :].astype(bf16)], axis=2
    )
    kv_pair = jnp.concatenate([kv_own, swap(kv_own, "row")], axis=1)
    kv_all = jnp.concatenate([kv_pair, swap(kv_pair, "col")], axis=1)
    query_rot = rotate(
        qkv_lin[..., :QD].reshape(seq_count, quarter, QH, HD), cosine, sine_term
    ).astype(bf16)
    key_rows, value_rows = split_kv(kv_all, seq_count, length)
    query_grp = query_rot.reshape(seq_count, quarter, KH, QH // KH, HD)
    scores = masked_scores(query_grp, key_rows, allowed)
    row_max = jnp.max(scores, axis=-1, keepdims=True)
    weights_exp = jnp.exp(scores - row_max)
    row_sum = jnp.sum(weights_exp, axis=-1, keepdims=True)
    log_total = row_max + jnp.log(row_sum)
    attn_probs = (weights_exp / row_sum).astype(bf16)
    attended = dot("shgqk,skhd->sqhgd", attn_probs, value_rows)
    attended = attended.reshape(seq_count, quarter, QD).astype(bf16)
    branch = dot("sqe,ed->sqd", attended, output_full).astype(bf16)
    middle = x_tok + branch.astype(jnp.float32)
    normed_second, root_second = norm_apply(middle, gain_full[1])

    second = normed_second.reshape(own_rows, D)
    dy_rows = dy_own.reshape(own_rows, D)
    rows = [second, swap(second, "col")]
    dys = [dy_rows, swap(dy_rows, "col")]
    gates = [dot("td,fd->tf", v, gate_full) for v in rows]
    ups = [dot("td,fd->tf", v, up_full) for v in rows]
    hiddens = [(jax.nn.silu(g) * u).astype(bf16) for g, u in zip(gates, ups)]

    def back(dy, gate_lin, up_lin):
        grad_hidden = dot("td,fd->tf", dy, down_full)
        sig = jax.nn.sigmoid(gate_lin)
        grad_gate = (grad_hidden * up_lin * sig * (1.0 + gate_lin * (1.0 - sig))).astype(bf16)
        return (grad_gate, (grad_hidden * gate_lin * sig).astype(bf16))

    backs = [back(*v) for v in zip(dys, gates, ups)]

    def input_back(pair):
        return dot("tf,fd->td", pair[0], gate_full) + dot("tf,fd->td", pair[1], up_full)

    second_away = swap(input_back(backs[1]).astype(bf16), "col").astype(jnp.float32)
    grad_second = (input_back(backs[0]) + second_away).astype(bf16)
    grad_second = grad_second.reshape(seq_count, quarter, D).astype(jnp.float32)
    out_away = swap(dot("tf,fd->td", hiddens[1], down_full).astype(bf16), "col")
    ffn_out = (dot("tf,fd->td", hiddens[0], down_full) + out_away.astype(jnp.float32)).astype(bf16)
    layer_tok = (
        middle + ffn_out.reshape(seq_count, quarter, D).astype(jnp.float32)
    ).astype(bf16)
    layer_out = to_features(layer_tok, row_index)

    def weight_part(side):
        row_cut = [half_of(v, side, 1) for v in rows]
        dy_cut = [half_of(v, side, 1) for v in dys]

        def one(tall, wide):
            return dot("tf,td->fd", tall[0], wide[0]) + dot("tf,td->fd", tall[1], wide[1])

        return [
            one([b[0] for b in backs], row_cut),
            one([b[1] for b in backs], row_cut),
            one(hiddens, dy_cut),
        ]

    away = [v.astype(bf16) for v in weight_part(1 - row_index)]
    arrived = [swap(v, "row") for v in away]
    kept = weight_part(row_index)

    grad_mid_norm, gain_second_part = norm_back(middle, root_second, gain_full[1], grad_second)
    grad_middle = dy_own.astype(jnp.float32) + grad_mid_norm
    grad_branch = grad_middle.astype(bf16)
    grad_branch, away, kept = lax.optimization_barrier((grad_branch, away, kept))
    ffn_part = jnp.concatenate(
        [(k + a.astype(jnp.float32)).astype(bf16) for k, a in zip(kept, arrived)], axis=0
    )
    output_part = dot("sqe,sqd->ed", attended, grad_branch)
    grad_attended = dot("sqd,ed->sqe", grad_branch, output_full).astype(bf16)
    exact_probs = jnp.exp(masked_scores(query_grp, key_rows, allowed) - log_total)
    grad_att_grp = grad_attended.reshape(seq_count, quarter, KH, QH // KH, HD)
    grad_probs = dot("sqhgd,skhd->shgqk", grad_att_grp, value_rows)
    row_delta = jnp.sum(exact_probs * grad_probs, axis=-1, keepdims=True)
    grad_scores = (exact_probs * (grad_probs - row_delta)).astype(bf16)
    grad_keys = dot("shgqk,sqhgd->skhd", grad_scores, query_grp) * HD ** (-0.5)
    grad_values = dot("shgqk,sqhgd->skhd", exact_probs.astype(bf16), grad_att_grp)
    grad_kv = jnp.concatenate(
        [grad_keys.reshape(seq_count, length, KD), grad_values.reshape(seq_count, length, KD)],
        axis=2,
    ).astype(bf16)
    near = 2 * quarter
    kv_sum = grad_kv[:, :near].astype(jnp.float32) + swap(grad_kv[:, near:], "col").astype(
        jnp.float32
    )
    grad_kv_own = kv_sum[:, :quarter] + swap(kv_sum[:, quarter:].astype(bf16), "row").astype(
        jnp.float32
    )
    grad_query_rot = dot("shgqk,skhd->sqhgd", grad_scores, key_rows) * HD ** (-0.5)
    grad_query_lin = (
        unrotate(grad_query_rot.reshape(seq_count, quarter, QH, HD), cosine, sine_term)
        .reshape(seq_count, quarter, QD)
        .astype(bf16)
    )
    grad_key_lin = (
        unrotate(grad_kv_own[..., :KD].reshape(seq_count, quarter, KH, HD), cosine, sine_term)
        .reshape(seq_count, quarter, KD)
        .astype(bf16)
    )
    grad_kv_lin = jnp.concatenate([grad_key_lin, grad_kv_own[..., KD:].astype(bf16)], axis=2)
    query_part = dot("sqd,sqe->de", first_tok, grad_query_lin)
    kv_part = dot("sqd,sqe->de", first_tok, grad_kv_lin)
    grad_first = dot("sqe,de->sqd", grad_query_lin, qkv_full[:, :QD]) + dot(
        "sqe,de->sqd", grad_kv_lin, qkv_full[:, QD:]
    )
    grad_first = grad_first.astype(bf16).astype(jnp.float32)
    grad_in_norm, gain_first_part = norm_back(x_tok, root_first, gain_full[0], grad_first)
    input_grad = to_features((grad_middle + grad_in_norm).astype(bf16), row_index).astype(
        jnp.float32
    )

    ffn_sum = dp_total(ffn_part, 0).astype(jnp.float32)
    qo_part = jnp.concatenate([query_part, output_part], axis=1)
    qo_sum = dp_total(scatter_rows(qo_part, row_index, col_index), 1).astype(jnp.float32)
    kv_grad = dp_total(scatter_rows(kv_part, row_index, col_index), 1).astype(jnp.float32)
    gain_sum = lax.psum(jnp.stack([gain_first_part, gain_second_part]), ("dp", "row", "col"))
    gain_sum = half_of(gain_sum, row_index, 1)
    return (
        layer_out,
        input_grad,
        gain_sum[0],
        qo_sum[:, :QD],
        kv_grad[:, :KD],
        kv_grad[:, KD:],
        qo_sum[:, QD:],
        gain_sum[1],
        ffn_sum[:units].T,
        ffn_sum[units : 2 * units].T,
        ffn_sum[2 * units :],
    )


def solution(mesh):
    placed = (
        P("dp", "col", "row"),
        P("dp", None),
        P("dp", None),
        P("row"),
        P(("row", "col"), None),
        P(("row", "col"), None),
        P(("row", "col"), None),
        P(("row", "col"), None),
        P("row"),
        P("row", "col"),
        P("row", "col"),
        P("col", "row"),
        P("dp", "col", "row"),
    )
    return jax.shard_map(
        local,
        mesh=mesh,
        in_specs=placed,
        out_specs=(
            P("dp", "col", "row"),
            P("dp", "col", "row"),
            P("row"),
            P(("row", "col"), None),
            P(("row", "col"), None),
            P(("row", "col"), None),
            P(("row", "col"), None),
            P("row"),
            P("row", "col"),
            P("row", "col"),
            P("col", "row"),
        ),
        check_vma=False,
    )
```

```python
import jax
import jax.numpy as jnp
from jax import lax
from jax.sharding import PartitionSpec as P

D = 960
QH = 15
KH = 5
HD = 64
QD = 960
KD = 320


eps_norm = 1e-05
rope_base = 10000.0
masked_value = -1e30


def swap(values, axis_name):
    size = lax.axis_size(axis_name)
    return lax.ppermute(values, axis_name, [(i, size - 1 - i) for i in range(size)])


def ordered(own, other, index, axis):
    return jnp.where(
        index == 0,
        jnp.concatenate([own, other], axis=axis),
        jnp.concatenate([other, own], axis=axis),
    )


def half_of(values, index, axis):
    size = values.shape[axis] // 2
    return lax.dynamic_slice_in_dim(values, index * size, size, axis)


def to_tokens(values, row_index):
    other = swap(half_of(values, 1 - row_index, 1), "row")
    return ordered(half_of(values, row_index, 1), other, row_index, 2)


def to_features(values, row_index):
    other = swap(half_of(values, 1 - row_index, 2), "row")
    return ordered(half_of(values, row_index, 2), other, row_index, 1)


def gather_rows(own, row_index, col_index):
    pair = ordered(own[None], swap(own, "row")[None], row_index, 0)
    full = ordered(pair[:, None], swap(pair, "col")[:, None], col_index, 1)
    return full.reshape(-1, own.shape[1])


def scatter_rows(part, row_index, col_index):
    blocks = part.reshape(2, 2, part.shape[0] // 4, part.shape[1])
    keep = half_of(blocks, col_index, 1)[:, 0]
    away = half_of(blocks, 1 - col_index, 1)[:, 0]
    pair = keep + swap(away.astype(jnp.bfloat16), "col").astype(jnp.float32)
    own = half_of(pair, row_index, 0)[0]
    send = half_of(pair, 1 - row_index, 0)[0]
    return own + swap(send.astype(jnp.bfloat16), "row").astype(jnp.float32)


def dp_total(values, dim):
    part = lax.psum_scatter(
        values.astype(jnp.bfloat16), "dp", scatter_dimension=dim, tiled=True
    )
    return lax.all_gather(part, "dp", axis=dim, tiled=True)


def xor_partner(values, step):
    size = lax.axis_size("dp")
    return lax.ppermute(values, "dp", [(i, i ^ step) for i in range(size)])


def dp_direct(values):
    size = lax.axis_size("dp")
    rows = values.shape[0]
    if size > 8 or size & (size - 1) or rows % size:
        return dp_total(values, 1)
    index = lax.axis_index("dp")
    piece = rows // size
    values = values.astype(jnp.bfloat16)

    def piece_of(step):
        return lax.dynamic_slice_in_dim(values, (index ^ step) * piece, piece, 0)

    total = piece_of(0).astype(jnp.float32)
    for part in [xor_partner(piece_of(step), step) for step in range(1, size)]:
        total = total + part.astype(jnp.float32)
    total = total.astype(jnp.bfloat16)
    pieces = jnp.stack([total] + [xor_partner(total, step) for step in range(1, size)])
    return jnp.concatenate(
        [lax.dynamic_index_in_dim(pieces, index ^ j, 0, keepdims=False) for j in range(size)],
        axis=0,
    )


def dp_small(values):
    size = lax.axis_size("dp")
    if size & (size - 1):
        return lax.psum(values, "dp")
    step = 1
    while step < size:
        values = values + xor_partner(values, step)
        step *= 2
    return values


def norm_apply(values, gain):
    inv_root = lax.rsqrt(jnp.mean(values * values, axis=-1, keepdims=True) + eps_norm)
    return ((values * inv_root * gain).astype(jnp.bfloat16), inv_root)


def norm_back(values, inv_root, gain, grad_normed):
    weighted = grad_normed * gain
    cross = jnp.sum(weighted * values, axis=-1, keepdims=True)
    grad_values = inv_root * weighted - values * inv_root**3 * cross / D
    gain_part = jnp.sum(grad_normed * values * inv_root, axis=(0, 1))
    return (grad_values, gain_part)


def dot(spec, left, right):
    return jnp.einsum(spec, left, right, preferred_element_type=jnp.float32)


def rotary(pos_rows):
    frequency = rope_base ** (-(jnp.arange(HD // 2, dtype=jnp.float32) * 2.0 / HD))
    angle_grid = pos_rows.astype(jnp.float32)[..., None] * frequency
    return (jnp.cos(angle_grid)[:, :, None, :], jnp.sin(angle_grid)[:, :, None, :])


def rotate(values, cosine, sine_term):
    half_dim = values.shape[-1] // 2
    lead_half = values[..., :half_dim]
    tail_half = values[..., half_dim:]
    return jnp.concatenate(
        [lead_half * cosine - tail_half * sine_term, tail_half * cosine + lead_half * sine_term],
        axis=-1,
    )


def unrotate(grads, cosine, sine_term):
    half_dim = grads.shape[-1] // 2
    lead_half = grads[..., :half_dim]
    tail_half = grads[..., half_dim:]
    return jnp.concatenate(
        [lead_half * cosine + tail_half * sine_term, tail_half * cosine - lead_half * sine_term],
        axis=-1,
    )


def masked_scores(query_grp, key_rows, allowed):
    scores = jnp.einsum(
        "sqhgd,skhd->shgqk", query_grp, key_rows, preferred_element_type=jnp.float32
    ) * HD ** (-0.5)
    return jnp.where(allowed[:, None, None], scores, masked_value)


def split_kv(kv_rows, seq_count, length):
    key_rows = kv_rows[..., :KD].reshape(seq_count, length, KH, HD)
    value_rows = kv_rows[..., KD:].reshape(seq_count, length, KH, HD)
    return (key_rows, value_rows)


def local(
    inputs,
    segments,
    positions,
    gain_first,
    query_weight,
    key_weight,
    value_weight,
    output_weight,
    gain_second,
    gate_weight,
    up_weight,
    down_weight,
    cotangent,
):
    seq_count, half_len, half_width = inputs.shape
    length = segments.shape[1]
    quarter = length // 4
    own_rows = seq_count * quarter
    dp_size = lax.axis_size("dp")
    dp_index = lax.axis_index("dp")
    row_index = lax.axis_index("row")
    col_index = lax.axis_index("col")
    bf16 = jnp.bfloat16


    own_ffn = jnp.stack([gate_weight.T, up_weight.T, down_weight])
    units = own_ffn.shape[1]
    piece = units // dp_size
    ffn_slice = jnp.stack(
        [
            lax.dynamic_slice_in_dim(gate_weight, dp_index * piece, piece, 1).T,
            lax.dynamic_slice_in_dim(up_weight, dp_index * piece, piece, 1).T,
            lax.dynamic_slice_in_dim(down_weight, dp_index * piece, piece, 0),
        ]
    )
    x_tok, other_slice = lax.optimization_barrier(
        (to_tokens(inputs, row_index), swap(ffn_slice, "row"))
    )
    x_tok = x_tok.astype(jnp.float32)
    qkv_full = gather_rows(
        jnp.concatenate([query_weight, key_weight, value_weight], axis=1), row_index, col_index
    )
    other_ffn = lax.all_gather(other_slice, "dp", axis=1, tiled=True)
    ffn_full = ordered(own_ffn, other_ffn, row_index, 2)
    gate_full, up_full, down_full = ffn_full[0], ffn_full[1], ffn_full[2]
    gain_own = jnp.stack([gain_first, gain_second])
    gain_full = ordered(gain_own, swap(gain_own, "row"), row_index, 1)

    starts = [
        (c * 2 + r) * quarter
        for c, r in (
            (col_index, row_index),
            (col_index, 1 - row_index),
            (1 - col_index, row_index),
            (1 - col_index, 1 - row_index),
        )
    ]
    span = jnp.arange(quarter, dtype=jnp.int32)
    query_pos = lax.dynamic_slice_in_dim(positions, starts[0], quarter, 1)
    query_seg = lax.dynamic_slice_in_dim(segments, starts[0], quarter, 1)
    key_seg = jnp.concatenate(
        [lax.dynamic_slice_in_dim(segments, s, quarter, 1) for s in starts], axis=1
    )
    key_order = jnp.concatenate([s + span for s in starts])
    query_order = starts[0] + span
    allowed = (query_seg[:, :, None] == key_seg[:, None, :]) & (
        key_order[None, None, :] <= query_order[None, :, None]
    )

    first_tok, root_first = norm_apply(x_tok, gain_full[0])
    qkv_lin = dot("sqd,de->sqe", first_tok, qkv_full)
    cosine, sine_term = rotary(query_pos)
    key_rot = rotate(
        qkv_lin[..., QD : QD + KD].reshape(seq_count, quarter, KH, HD), cosine, sine_term
    ).astype(bf16)
    kv_own = jnp.concatenate(
        [key_rot.reshape(seq_count, quarter, KD), qkv_lin[..., QD + KD :].astype(bf16)], axis=2
    )
    kv_pair = jnp.concatenate([kv_own, swap(kv_own, "row")], axis=1)
    kv_pair, later_weight, later_dy = lax.optimization_barrier(
        (kv_pair, output_weight, cotangent)
    )
    output_full = gather_rows(later_weight, row_index, col_index)
    dy_own = to_tokens(later_dy, row_index)
    kv_all = jnp.concatenate([kv_pair, swap(kv_pair, "col")], axis=1)
    query_rot = rotate(
        qkv_lin[..., :QD].reshape(seq_count, quarter, QH, HD), cosine, sine_term
    ).astype(bf16)
    key_rows, value_rows = split_kv(kv_all, seq_count, length)
    query_grp = query_rot.reshape(seq_count, quarter, KH, QH // KH, HD)
    scores = masked_scores(query_grp, key_rows, allowed)
    row_max = jnp.max(scores, axis=-1, keepdims=True)
    weights_exp = jnp.exp(scores - row_max)
    row_sum = jnp.sum(weights_exp, axis=-1, keepdims=True)
    log_total = row_max + jnp.log(row_sum)
    attn_probs = (weights_exp / row_sum).astype(bf16)
    attended = dot("shgqk,skhd->sqhgd", attn_probs, value_rows)
    attended = attended.reshape(seq_count, quarter, QD).astype(bf16)
    branch = dot("sqe,ed->sqd", attended, output_full).astype(bf16)
    middle = x_tok + branch.astype(jnp.float32)
    normed_second, root_second = norm_apply(middle, gain_full[1])

    second = normed_second.reshape(own_rows, D)
    dy_rows = dy_own.reshape(own_rows, D)
    rows = [second, swap(second, "col")]
    dys = [dy_rows, swap(dy_rows, "col")]
    gates = [dot("td,fd->tf", v, gate_full) for v in rows]
    ups = [dot("td,fd->tf", v, up_full) for v in rows]
    hiddens = [(jax.nn.silu(g) * u).astype(bf16) for g, u in zip(gates, ups)]

    def back(dy, gate_lin, up_lin):
        grad_hidden = dot("td,fd->tf", dy, down_full)
        sig = jax.nn.sigmoid(gate_lin)
        grad_gate = (grad_hidden * up_lin * sig * (1.0 + gate_lin * (1.0 - sig))).astype(bf16)
        return (grad_gate, (grad_hidden * gate_lin * sig).astype(bf16))

    backs = [back(*v) for v in zip(dys, gates, ups)]

    def input_back(pair):
        return dot("tf,fd->td", pair[0], gate_full) + dot("tf,fd->td", pair[1], up_full)

    second_away = swap(input_back(backs[1]).astype(bf16), "col").astype(jnp.float32)
    grad_second = (input_back(backs[0]) + second_away).astype(bf16)
    grad_second = grad_second.reshape(seq_count, quarter, D).astype(jnp.float32)
    out_away = swap(dot("tf,fd->td", hiddens[1], down_full).astype(bf16), "col")
    ffn_out = (dot("tf,fd->td", hiddens[0], down_full) + out_away.astype(jnp.float32)).astype(bf16)
    layer_tok = (
        middle + ffn_out.reshape(seq_count, quarter, D).astype(jnp.float32)
    ).astype(bf16)
    layer_out = to_features(layer_tok, row_index)

    def weight_part(side):
        row_cut = [half_of(v, side, 1) for v in rows]
        dy_cut = [half_of(v, side, 1) for v in dys]

        def one(tall, wide):
            return dot("tf,td->fd", tall[0], wide[0]) + dot("tf,td->fd", tall[1], wide[1])

        return [
            one([b[0] for b in backs], row_cut),
            one([b[1] for b in backs], row_cut),
            one(hiddens, dy_cut),
        ]

    away = [v.astype(bf16) for v in weight_part(1 - row_index)]
    arrived = [swap(v, "row") for v in away]
    kept = weight_part(row_index)

    grad_mid_norm, gain_second_part = norm_back(middle, root_second, gain_full[1], grad_second)
    grad_middle = dy_own.astype(jnp.float32) + grad_mid_norm
    grad_branch = grad_middle.astype(bf16)
    grad_branch, away, kept = lax.optimization_barrier((grad_branch, away, kept))
    ffn_part = jnp.concatenate(
        [(k + a.astype(jnp.float32)).astype(bf16) for k, a in zip(kept, arrived)], axis=0
    )
    output_part = dot("sqe,sqd->ed", attended, grad_branch)
    grad_attended = dot("sqd,ed->sqe", grad_branch, output_full).astype(bf16)
    exact_probs = jnp.exp(masked_scores(query_grp, key_rows, allowed) - log_total)
    grad_att_grp = grad_attended.reshape(seq_count, quarter, KH, QH // KH, HD)
    grad_probs = dot("sqhgd,skhd->shgqk", grad_att_grp, value_rows)
    row_delta = jnp.sum(exact_probs * grad_probs, axis=-1, keepdims=True)
    grad_scores = (exact_probs * (grad_probs - row_delta)).astype(bf16)
    grad_keys = dot("shgqk,sqhgd->skhd", grad_scores, query_grp) * HD ** (-0.5)
    grad_values = dot("shgqk,sqhgd->skhd", exact_probs.astype(bf16), grad_att_grp)
    grad_kv = jnp.concatenate(
        [grad_keys.reshape(seq_count, length, KD), grad_values.reshape(seq_count, length, KD)],
        axis=2,
    ).astype(bf16)
    near = 2 * quarter
    kv_sum = grad_kv[:, :near].astype(jnp.float32) + swap(grad_kv[:, near:], "col").astype(
        jnp.float32
    )
    grad_kv_own = kv_sum[:, :quarter] + swap(kv_sum[:, quarter:].astype(bf16), "row").astype(
        jnp.float32
    )
    grad_query_rot = dot("shgqk,skhd->sqhgd", grad_scores, key_rows) * HD ** (-0.5)
    grad_query_lin = (
        unrotate(grad_query_rot.reshape(seq_count, quarter, QH, HD), cosine, sine_term)
        .reshape(seq_count, quarter, QD)
        .astype(bf16)
    )
    grad_key_lin = (
        unrotate(grad_kv_own[..., :KD].reshape(seq_count, quarter, KH, HD), cosine, sine_term)
        .reshape(seq_count, quarter, KD)
        .astype(bf16)
    )
    grad_kv_lin = jnp.concatenate([grad_key_lin, grad_kv_own[..., KD:].astype(bf16)], axis=2)
    query_part = dot("sqd,sqe->de", first_tok, grad_query_lin)
    kv_part = dot("sqd,sqe->de", first_tok, grad_kv_lin)
    grad_first = dot("sqe,de->sqd", grad_query_lin, qkv_full[:, :QD]) + dot(
        "sqe,de->sqd", grad_kv_lin, qkv_full[:, QD:]
    )
    grad_first = grad_first.astype(bf16).astype(jnp.float32)
    grad_in_norm, gain_first_part = norm_back(x_tok, root_first, gain_full[0], grad_first)
    input_grad = to_features((grad_middle + grad_in_norm).astype(bf16), row_index).astype(
        jnp.float32
    )

    ffn_sum = dp_total(ffn_part, 0).astype(jnp.float32)
    qo_part = jnp.concatenate([query_part, output_part], axis=1)
    qo_sum = dp_direct(scatter_rows(qo_part, row_index, col_index)).astype(jnp.float32)
    kv_grad = dp_direct(scatter_rows(kv_part, row_index, col_index)).astype(jnp.float32)
    gain_part = jnp.stack([gain_first_part, gain_second_part])
    gain_sum = half_of(gain_part, row_index, 1) + swap(half_of(gain_part, 1 - row_index, 1), "row")
    gain_sum = dp_small(gain_sum + swap(gain_sum, "col"))
    return (
        layer_out,
        input_grad,
        gain_sum[0],
        qo_sum[:, :QD],
        kv_grad[:, :KD],
        kv_grad[:, KD:],
        qo_sum[:, QD:],
        gain_sum[1],
        ffn_sum[:units].T,
        ffn_sum[units : 2 * units].T,
        ffn_sum[2 * units :],
    )


def solution(mesh):
    placed = (
        P("dp", "col", "row"),
        P("dp", None),
        P("dp", None),
        P("row"),
        P(("row", "col"), None),
        P(("row", "col"), None),
        P(("row", "col"), None),
        P(("row", "col"), None),
        P("row"),
        P("row", "col"),
        P("row", "col"),
        P("col", "row"),
        P("dp", "col", "row"),
    )
    return jax.shard_map(
        local,
        mesh=mesh,
        in_specs=placed,
        out_specs=(
            P("dp", "col", "row"),
            P("dp", "col", "row"),
            P("row"),
            P(("row", "col"), None),
            P(("row", "col"), None),
            P(("row", "col"), None),
            P(("row", "col"), None),
            P("row"),
            P("row", "col"),
            P("row", "col"),
            P("col", "row"),
        ),
        check_vma=False,
    )
```

```python
import jax
import jax.numpy as jnp
from jax import lax
from jax.sharding import PartitionSpec as P

D = 960
QH = 15
KH = 5
HD = 64
QD = 960
KD = 320


eps_norm = 1e-05
rope_base = 10000.0
masked_value = -1e30


def swap(values, axis_name):
    size = lax.axis_size(axis_name)
    return lax.ppermute(values, axis_name, [(i, size - 1 - i) for i in range(size)])


def ordered(own, other, index, axis):
    return jnp.where(
        index == 0,
        jnp.concatenate([own, other], axis=axis),
        jnp.concatenate([other, own], axis=axis),
    )


def half_of(values, index, axis):
    size = values.shape[axis] // 2
    return lax.dynamic_slice_in_dim(values, index * size, size, axis)


def to_tokens(values, row_index):
    other = swap(half_of(values, 1 - row_index, 1), "row")
    return ordered(half_of(values, row_index, 1), other, row_index, 2)


def to_features(values, row_index):
    other = swap(half_of(values, 1 - row_index, 2), "row")
    return ordered(half_of(values, row_index, 2), other, row_index, 1)


def gather_rows(own, row_index, col_index):
    pair = ordered(own[None], swap(own, "row")[None], row_index, 0)
    full = ordered(pair[:, None], swap(pair, "col")[:, None], col_index, 1)
    return full.reshape(-1, own.shape[1])


def scatter_rows(part, row_index, col_index):
    blocks = part.reshape(2, 2, part.shape[0] // 4, part.shape[1])
    keep = half_of(blocks, col_index, 1)[:, 0]
    away = half_of(blocks, 1 - col_index, 1)[:, 0]
    pair = keep + swap(away.astype(jnp.bfloat16), "col").astype(jnp.float32)
    own = half_of(pair, row_index, 0)[0]
    send = half_of(pair, 1 - row_index, 0)[0]
    return own + swap(send.astype(jnp.bfloat16), "row").astype(jnp.float32)


def dp_total(values, dim):
    part = lax.psum_scatter(
        values.astype(jnp.bfloat16), "dp", scatter_dimension=dim, tiled=True
    )
    return lax.all_gather(part, "dp", axis=dim, tiled=True)


def xor_partner(values, step):
    size = lax.axis_size("dp")
    return lax.ppermute(values, "dp", [(i, i ^ step) for i in range(size)])


def dp_direct(values):
    size = lax.axis_size("dp")
    rows = values.shape[0]
    if size > 8 or size & (size - 1) or rows % size:
        return dp_total(values, 1)
    index = lax.axis_index("dp")
    piece = rows // size
    values = values.astype(jnp.bfloat16)

    def piece_of(step):
        return lax.dynamic_slice_in_dim(values, (index ^ step) * piece, piece, 0)

    total = piece_of(0).astype(jnp.float32)
    for part in [xor_partner(piece_of(step), step) for step in range(1, size)]:
        total = total + part.astype(jnp.float32)
    total = total.astype(jnp.bfloat16)
    pieces = jnp.stack([total] + [xor_partner(total, step) for step in range(1, size)])
    return jnp.concatenate(
        [lax.dynamic_index_in_dim(pieces, index ^ j, 0, keepdims=False) for j in range(size)],
        axis=0,
    )


def dp_small(values):
    size = lax.axis_size("dp")
    if size & (size - 1):
        return lax.psum(values, "dp")
    step = 1
    while step < size:
        values = values + xor_partner(values, step)
        step *= 2
    return values


def norm_apply(values, gain):
    inv_root = lax.rsqrt(jnp.mean(values * values, axis=-1, keepdims=True) + eps_norm)
    return ((values * inv_root * gain).astype(jnp.bfloat16), inv_root)


def norm_back(values, inv_root, gain, grad_normed):
    weighted = grad_normed * gain
    cross = jnp.sum(weighted * values, axis=-1, keepdims=True)
    grad_values = inv_root * weighted - values * inv_root**3 * cross / D
    gain_part = jnp.sum(grad_normed * values * inv_root, axis=(0, 1))
    return (grad_values, gain_part)


def dot(spec, left, right):
    return jnp.einsum(spec, left, right, preferred_element_type=jnp.float32)


def rotary(pos_rows):
    frequency = rope_base ** (-(jnp.arange(HD // 2, dtype=jnp.float32) * 2.0 / HD))
    angle_grid = pos_rows.astype(jnp.float32)[..., None] * frequency
    return (jnp.cos(angle_grid)[:, :, None, :], jnp.sin(angle_grid)[:, :, None, :])


def rotate(values, cosine, sine_term):
    half_dim = values.shape[-1] // 2
    lead_half = values[..., :half_dim]
    tail_half = values[..., half_dim:]
    return jnp.concatenate(
        [lead_half * cosine - tail_half * sine_term, tail_half * cosine + lead_half * sine_term],
        axis=-1,
    )


def unrotate(grads, cosine, sine_term):
    half_dim = grads.shape[-1] // 2
    lead_half = grads[..., :half_dim]
    tail_half = grads[..., half_dim:]
    return jnp.concatenate(
        [lead_half * cosine + tail_half * sine_term, tail_half * cosine - lead_half * sine_term],
        axis=-1,
    )


def masked_scores(query_grp, key_rows, allowed):
    scores = jnp.einsum(
        "sqhgd,skhd->shgqk", query_grp, key_rows, preferred_element_type=jnp.float32
    ) * HD ** (-0.5)
    return jnp.where(allowed[:, None, None], scores, masked_value)


def split_kv(kv_rows, seq_count, length):
    key_rows = kv_rows[..., :KD].reshape(seq_count, length, KH, HD)
    value_rows = kv_rows[..., KD:].reshape(seq_count, length, KH, HD)
    return (key_rows, value_rows)


def local(
    inputs,
    segments,
    positions,
    gain_first,
    query_weight,
    key_weight,
    value_weight,
    output_weight,
    gain_second,
    gate_weight,
    up_weight,
    down_weight,
    cotangent,
):
    seq_count, half_len, half_width = inputs.shape
    length = segments.shape[1]
    quarter = length // 4
    own_rows = seq_count * quarter
    dp_size = lax.axis_size("dp")
    dp_index = lax.axis_index("dp")
    row_index = lax.axis_index("row")
    col_index = lax.axis_index("col")
    bf16 = jnp.bfloat16


    own_ffn = jnp.stack([gate_weight.T, up_weight.T, down_weight])
    units = own_ffn.shape[1]
    piece = units // dp_size
    ffn_slice = jnp.stack(
        [
            lax.dynamic_slice_in_dim(gate_weight, dp_index * piece, piece, 1).T,
            lax.dynamic_slice_in_dim(up_weight, dp_index * piece, piece, 1).T,
            lax.dynamic_slice_in_dim(down_weight, dp_index * piece, piece, 0),
        ]
    )
    x_tok, other_slice = lax.optimization_barrier(
        (to_tokens(inputs, row_index), swap(ffn_slice, "row"))
    )
    x_tok = x_tok.astype(jnp.float32)
    qkv_full = gather_rows(
        jnp.concatenate([query_weight, key_weight, value_weight], axis=1), row_index, col_index
    )
    other_ffn = lax.all_gather(other_slice, "dp", axis=1, tiled=True)
    ffn_full = ordered(own_ffn, other_ffn, row_index, 2)
    gate_full, up_full, down_full = ffn_full[0], ffn_full[1], ffn_full[2]
    gain_own = jnp.stack([gain_first, gain_second])
    gain_full = ordered(gain_own, swap(gain_own, "row"), row_index, 1)

    starts = [
        (c * 2 + r) * quarter
        for c, r in (
            (col_index, row_index),
            (col_index, 1 - row_index),
            (1 - col_index, row_index),
            (1 - col_index, 1 - row_index),
        )
    ]
    span = jnp.arange(quarter, dtype=jnp.int32)
    query_pos = lax.dynamic_slice_in_dim(positions, starts[0], quarter, 1)
    query_seg = lax.dynamic_slice_in_dim(segments, starts[0], quarter, 1)
    key_seg = jnp.concatenate(
        [lax.dynamic_slice_in_dim(segments, s, quarter, 1) for s in starts], axis=1
    )
    key_order = jnp.concatenate([s + span for s in starts])
    query_order = starts[0] + span
    allowed = (query_seg[:, :, None] == key_seg[:, None, :]) & (
        key_order[None, None, :] <= query_order[None, :, None]
    )

    first_tok, root_first = norm_apply(x_tok, gain_full[0])
    qkv_lin = dot("sqd,de->sqe", first_tok, qkv_full)
    cosine, sine_term = rotary(query_pos)
    key_rot = rotate(
        qkv_lin[..., QD : QD + KD].reshape(seq_count, quarter, KH, HD), cosine, sine_term
    ).astype(bf16)
    kv_own = jnp.concatenate(
        [key_rot.reshape(seq_count, quarter, KD), qkv_lin[..., QD + KD :].astype(bf16)], axis=2
    )
    kv_pair = jnp.concatenate([kv_own, swap(kv_own, "row")], axis=1)
    kv_pair, later_weight, later_dy = lax.optimization_barrier(
        (kv_pair, output_weight, cotangent)
    )
    output_full = gather_rows(later_weight, row_index, col_index)
    dy_own = to_tokens(later_dy, row_index)
    kv_all = jnp.concatenate([kv_pair, swap(kv_pair, "col")], axis=1)
    query_rot = rotate(
        qkv_lin[..., :QD].reshape(seq_count, quarter, QH, HD), cosine, sine_term
    ).astype(bf16)
    key_rows, value_rows = split_kv(kv_all, seq_count, length)
    query_grp = query_rot.reshape(seq_count, quarter, KH, QH // KH, HD)
    scores = masked_scores(query_grp, key_rows, allowed)
    row_max = jnp.max(scores, axis=-1, keepdims=True)
    weights_exp = jnp.exp(scores - row_max)
    row_sum = jnp.sum(weights_exp, axis=-1, keepdims=True)
    log_total = row_max + jnp.log(row_sum)
    attn_probs = (weights_exp / row_sum).astype(bf16)
    attended = dot("shgqk,skhd->sqhgd", attn_probs, value_rows)
    attended = attended.reshape(seq_count, quarter, QD).astype(bf16)
    branch = dot("sqe,ed->sqd", attended, output_full).astype(bf16)
    middle = x_tok + branch.astype(jnp.float32)
    normed_second, root_second = norm_apply(middle, gain_full[1])

    second = normed_second.reshape(own_rows, D)
    dy_rows = dy_own.reshape(own_rows, D)
    rows = [second, swap(second, "col")]
    dys = [dy_rows, swap(dy_rows, "col")]
    gates = [dot("td,fd->tf", v, gate_full) for v in rows]
    ups = [dot("td,fd->tf", v, up_full) for v in rows]
    hiddens = [(jax.nn.silu(g) * u).astype(bf16) for g, u in zip(gates, ups)]

    def back(dy, gate_lin, up_lin):
        grad_hidden = dot("td,fd->tf", dy, down_full)
        sig = jax.nn.sigmoid(gate_lin)
        grad_gate = (grad_hidden * up_lin * sig * (1.0 + gate_lin * (1.0 - sig))).astype(bf16)
        return (grad_gate, (grad_hidden * gate_lin * sig).astype(bf16))

    backs = [back(*v) for v in zip(dys, gates, ups)]

    def input_back(pair):
        return dot("tf,fd->td", pair[0], gate_full) + dot("tf,fd->td", pair[1], up_full)

    second_away = swap(input_back(backs[1]).astype(bf16), "col").astype(jnp.float32)
    grad_second = (input_back(backs[0]) + second_away).astype(bf16)
    grad_second = grad_second.reshape(seq_count, quarter, D).astype(jnp.float32)
    out_away = swap(dot("tf,fd->td", hiddens[1], down_full).astype(bf16), "col")
    ffn_out = (dot("tf,fd->td", hiddens[0], down_full) + out_away.astype(jnp.float32)).astype(bf16)
    layer_tok = (
        middle + ffn_out.reshape(seq_count, quarter, D).astype(jnp.float32)
    ).astype(bf16)
    layer_out = to_features(layer_tok, row_index)

    def weight_part(side):
        row_cut = [half_of(v, side, 1) for v in rows]
        dy_cut = [half_of(v, side, 1) for v in dys]

        def one(tall, wide):
            return dot("tf,td->fd", tall[0], wide[0]) + dot("tf,td->fd", tall[1], wide[1])

        return [
            one([b[0] for b in backs], row_cut),
            one([b[1] for b in backs], row_cut),
            one(hiddens, dy_cut),
        ]

    away = [v.astype(bf16) for v in weight_part(1 - row_index)]
    arrived = [swap(v, "row") for v in away]
    kept = weight_part(row_index)

    grad_mid_norm, gain_second_part = norm_back(middle, root_second, gain_full[1], grad_second)
    grad_middle = dy_own.astype(jnp.float32) + grad_mid_norm
    grad_branch = grad_middle.astype(bf16)
    grad_branch, away, kept = lax.optimization_barrier((grad_branch, away, kept))
    ffn_part = jnp.concatenate(
        [(k + a.astype(jnp.float32)).astype(bf16) for k, a in zip(kept, arrived)], axis=0
    )
    output_part = dot("sqe,sqd->ed", attended, grad_branch)
    grad_attended = dot("sqd,ed->sqe", grad_branch, output_full).astype(bf16)
    exact_probs = jnp.exp(masked_scores(query_grp, key_rows, allowed) - log_total)
    grad_att_grp = grad_attended.reshape(seq_count, quarter, KH, QH // KH, HD)
    grad_probs = dot("sqhgd,skhd->shgqk", grad_att_grp, value_rows)
    row_delta = jnp.sum(exact_probs * grad_probs, axis=-1, keepdims=True)
    grad_scores = (exact_probs * (grad_probs - row_delta)).astype(bf16)
    grad_scores, ffn_part = lax.optimization_barrier((grad_scores, ffn_part))
    ffn_piece = lax.psum_scatter(ffn_part, "dp", scatter_dimension=0, tiled=True)
    grad_keys = dot("shgqk,sqhgd->skhd", grad_scores, query_grp) * HD ** (-0.5)
    grad_values = dot("shgqk,sqhgd->skhd", exact_probs.astype(bf16), grad_att_grp)
    grad_kv = jnp.concatenate(
        [grad_keys.reshape(seq_count, length, KD), grad_values.reshape(seq_count, length, KD)],
        axis=2,
    ).astype(bf16)
    near = 2 * quarter
    kv_sum = grad_kv[:, :near].astype(jnp.float32) + swap(grad_kv[:, near:], "col").astype(
        jnp.float32
    )
    grad_kv_own = kv_sum[:, :quarter] + swap(kv_sum[:, quarter:].astype(bf16), "row").astype(
        jnp.float32
    )
    grad_query_rot = dot("shgqk,skhd->sqhgd", grad_scores, key_rows) * HD ** (-0.5)
    grad_query_lin = (
        unrotate(grad_query_rot.reshape(seq_count, quarter, QH, HD), cosine, sine_term)
        .reshape(seq_count, quarter, QD)
        .astype(bf16)
    )
    grad_key_lin = (
        unrotate(grad_kv_own[..., :KD].reshape(seq_count, quarter, KH, HD), cosine, sine_term)
        .reshape(seq_count, quarter, KD)
        .astype(bf16)
    )
    grad_kv_lin = jnp.concatenate([grad_key_lin, grad_kv_own[..., KD:].astype(bf16)], axis=2)
    grad_kv_lin, ffn_piece = lax.optimization_barrier((grad_kv_lin, ffn_piece))
    query_part = dot("sqd,sqe->de", first_tok, grad_query_lin)
    kv_part = dot("sqd,sqe->de", first_tok, grad_kv_lin)
    grad_first = dot("sqe,de->sqd", grad_query_lin, qkv_full[:, :QD]) + dot(
        "sqe,de->sqd", grad_kv_lin, qkv_full[:, QD:]
    )
    grad_first = grad_first.astype(bf16).astype(jnp.float32)
    grad_in_norm, gain_first_part = norm_back(x_tok, root_first, gain_full[0], grad_first)
    input_grad = to_features((grad_middle + grad_in_norm).astype(bf16), row_index).astype(
        jnp.float32
    )

    ffn_sum = lax.all_gather(ffn_piece, "dp", axis=0, tiled=True).astype(jnp.float32)
    qo_part = jnp.concatenate([query_part, output_part], axis=1)
    qo_sum = dp_direct(scatter_rows(qo_part, row_index, col_index)).astype(jnp.float32)
    kv_grad = dp_direct(scatter_rows(kv_part, row_index, col_index)).astype(jnp.float32)
    gain_part = jnp.stack([gain_first_part, gain_second_part])
    gain_sum = half_of(gain_part, row_index, 1) + swap(half_of(gain_part, 1 - row_index, 1), "row")
    gain_sum = dp_small(gain_sum + swap(gain_sum, "col"))
    return (
        layer_out,
        input_grad,
        gain_sum[0],
        qo_sum[:, :QD],
        kv_grad[:, :KD],
        kv_grad[:, KD:],
        qo_sum[:, QD:],
        gain_sum[1],
        ffn_sum[:units].T,
        ffn_sum[units : 2 * units].T,
        ffn_sum[2 * units :],
    )


def solution(mesh):
    placed = (
        P("dp", "col", "row"),
        P("dp", None),
        P("dp", None),
        P("row"),
        P(("row", "col"), None),
        P(("row", "col"), None),
        P(("row", "col"), None),
        P(("row", "col"), None),
        P("row"),
        P("row", "col"),
        P("row", "col"),
        P("col", "row"),
        P("dp", "col", "row"),
    )
    return jax.shard_map(
        local,
        mesh=mesh,
        in_specs=placed,
        out_specs=(
            P("dp", "col", "row"),
            P("dp", "col", "row"),
            P("row"),
            P(("row", "col"), None),
            P(("row", "col"), None),
            P(("row", "col"), None),
            P(("row", "col"), None),
            P("row"),
            P("row", "col"),
            P("row", "col"),
            P("col", "row"),
        ),
        check_vma=False,
    )
```
